128 devices in a mesh: wave: 32 (over y, x, core), lev: 4 (over z).
Axes of the slice: x: 4, y: 4, z: 4, core: 2. Of those that a mesh axis runs over, the one named last changes fastest.
Arguments:
- legendre: bfloat16 [1280, 1280, 128], P('wave'), may hold values from -0.15625 to 0.15625
- spectral: bfloat16 [1280, 1280, 288], P('wave', None, 'lev'), may hold values from -0.119628906 to 0.119628906
- slot_wave: int32 [1280], P('wave'), may hold values from 0 to 1279, as said below
- band_rows: int32 [256], P(('wave', 'lev')), may hold values from 0 to 255, as said below
- lon_count: int32 [256], P(('wave', 'lev')), may hold values from 20 to 5136, as said below
Outputs:
- grid: float32 [256, 144, 5136], P(('wave', 'lev'))
The draws below stay inside these ranges and needn't reach their ends.
Inputs may be any that keep to these rules, and one draw needn't show every extreme that they name: slot_wave is a permutation of the wavenumbers; the 40 slots of each index of wave hold 40 consecutive wavenumbers in some order, and which run each index holds is drawn. band_rows is a permutation of the window latitudes. Each northern window latitude has a distance index i from the pole (0 to 1279, indices may repeat), and lon_count[r] = 20 + 4 i for the latitude band_rows[r] mod 128, so a row and its mirror have the same count.
All inputs are finite; a program needn't handle non-finite values.
Results may differ from the reference program's by a relative error of at most 0.0065.
Values sent between devices are 32-bit elements; how exact they have to be, the bound alone decides.
A program may use at most 128 MiB of HBM per device.

```python
import math
import jax
import jax.numpy as jnp
from jax import lax

SLOT_DEV = 40
FLEV = 144
MW = 1280
NN = 1280
LATN = 128
LAT_ALL = 256
LONS = 5136


def row_order(key):
    return jax.random.permutation(key, LAT_ALL).astype(jnp.int32)


def draw_slot_wave(key, part):
    key = jax.random.fold_in(key, 11)
    first, second = jax.random.split(key)
    groups = MW // SLOT_DEV
    order = jax.random.permutation(first, groups)
    scores = jax.random.randint(second, (groups, SLOT_DEV), 0, 1 << 20) * SLOT_DEV + jnp.arange(SLOT_DEV, dtype=jnp.int32)[None, :]
    inner = jnp.argsort(scores, axis=1)
    return (order[:, None] * SLOT_DEV + inner).reshape(-1).astype(jnp.int32)


def draw_band_rows(key, part):
    rows = row_order(key)
    return rows


def draw_lon_count(key, part):
    rows = row_order(key)
    key = jax.random.fold_in(key, 23)
    first, second = jax.random.split(key)
    cycle = jax.random.randint(first, (LATN,), 0, MW)
    spots = jax.random.permutation(second, LATN)
    cycle = cycle.at[spots[0]].set(MW - 1)
    cycle = cycle.at[spots[1]].set(0)
    counts = (4 * cycle + 20).astype(jnp.int32)
    return jnp.take(counts, rows % LATN).astype(jnp.int32)


def shard_levels(own_key, extent, cuts, least, largest):
    factor_of = 1.0
    for position, shards_of in cuts:
        steps = jax.random.uniform(jax.random.fold_in(jax.random.fold_in(own_key, 6), position), (shards_of,), jnp.float32, least / len(cuts), largest / len(cuts))
        factor_of = factor_of * jnp.repeat(jnp.exp(steps), extent[position] // shards_of).reshape((-1,) + (1,) * (len(extent) - 1 - position))
    return factor_of


def normal_values(key, shape, deviation, reach, cuts=(), kind=jnp.bfloat16):
    gain = shard_levels(key, shape, cuts, -0.22, 0.18) if cuts else 1.0
    values = jax.random.normal(key, shape, jnp.float32) * deviation * gain
    return jnp.minimum(jnp.maximum(values, -reach), reach).astype(kind)


def setup_inputs(seed: int = 0) -> dict:
    splits = jax.random.split(jax.random.key(seed), 6)
    legendre = normal_values(splits[0], (MW, NN, LATN), NN ** -0.5, 0.15625, ((0, 32),))
    spectral = normal_values(splits[1], (MW, NN, 2 * FLEV), 0.02, 0.119628906, ((0, 32), (2, 4)))
    slot_wave = draw_slot_wave(jax.random.fold_in(splits[5], 71), 0)
    band_rows = draw_band_rows(jax.random.fold_in(splits[5], 71), 0)
    lon_count = draw_lon_count(jax.random.fold_in(splits[5], 71), 0)
    return dict(legendre=legendre, spectral=spectral, slot_wave=slot_wave, band_rows=band_rows, lon_count=lon_count)


TWO_PI = 2.0 * math.pi


def fourier_table(waves, number, longitude):
    phase = (waves[:, None] * longitude[None, :]) % number
    angle = phase.astype(jnp.float32) * (TWO_PI / number.astype(jnp.float32))
    weight = jnp.where(waves == 0, 1.0, 2.0).astype(jnp.float32)
    weight = jnp.where(2 * waves < number, weight, 0.0)
    inside = (longitude < number).astype(jnp.float32)
    cosine = weight[:, None] * jnp.cos(angle) * inside[None, :]
    sine = -weight[:, None] * jnp.sin(angle) * inside[None, :]
    return jnp.stack([cosine, sine], axis=1)


def reference(legendre, spectral, slot_wave, band_rows, lon_count):
    depth_index = jnp.arange(NN, dtype=jnp.int32)

    def one_slot(items):
        poles, coefficient, wave = items
        usable = depth_index < (NN - wave)
        even_mask = usable & (depth_index % 2 == 0)
        odd_mask = usable & (depth_index % 2 == 1)
        poles_wide = poles.astype(jnp.float32)
        values = coefficient.astype(jnp.float32)
        even_sum = jnp.dot(poles_wide.T, jnp.where(even_mask[:, None], values, 0.0),
                           precision=lax.Precision.HIGHEST, preferred_element_type=jnp.float32)
        odd_sum = jnp.dot(poles_wide.T, jnp.where(odd_mask[:, None], values, 0.0),
                          precision=lax.Precision.HIGHEST, preferred_element_type=jnp.float32)
        return jnp.concatenate([even_sum + odd_sum, even_sum - odd_sum], axis=0)

    fourier = lax.map(one_slot, (legendre, spectral, slot_wave))
    longitude = jnp.arange(LONS, dtype=jnp.int32)

    def one_row(items):
        latitude, number = items
        values = lax.dynamic_index_in_dim(fourier, latitude, 1, keepdims=False)
        left = values.reshape(MW, FLEV, 2).transpose(1, 0, 2).reshape(FLEV, 2 * MW)
        right = fourier_table(slot_wave, number, longitude).reshape(2 * MW, LONS).astype(jnp.bfloat16)
        right = lax.optimization_barrier(right).astype(jnp.float32)
        return jnp.dot(left, right, precision=lax.Precision.HIGHEST, preferred_element_type=jnp.float32)

    return lax.map(one_row, (band_rows, lon_count))
```

```python
import functools
import math

import jax
import jax.numpy as jnp
import numpy as np
from jax import lax
from jax.experimental import pallas as pl
from jax.experimental.pallas import tpu as pltpu
from jax.sharding import PartitionSpec as P

MESH = pl.DeviceIdType.MESH
F32 = jnp.float32
BF16 = jnp.bfloat16

SLOTS = 40
DEPTH = 1280
NORTH = 128
COLS = 72
FIELDS = 144
CHUNKS = 5
TILES = 9
PITCH = 16
PEERS = 128
WIDTH = 1536
RE_ROWS = 576
IM_ROWS = 432
LONS = 5136


def place():
    wave = lax.axis_index("wave")
    return wave // 8, (wave // 2) % 4, wave % 2, lax.axis_index("lev")


def order_of(y, x, core, z):
    return ((core * 4 + z) * 4 + x) * 4 + y


def neighbour(here, offset):
    y = lax.rem(here[0] + offset[0], 4)
    x = lax.rem(here[1] + offset[1], 4)
    core = lax.rem(here[2] + offset[2], 2)
    z = lax.rem(here[3] + offset[3], 4)
    return ((y * 4 + x) * 2 + core, z), order_of(y, x, core, z)


PLANE = [(y, x, 0, 0) for y in range(4) for x in range(4) if y or x]
LINE = [(0, 0, core, z) for core in range(2) for z in range(4) if core or z]


def placement_matrix():
    out = np.zeros((RE_ROWS, 1024), np.float32)
    for row in range(RE_ROWS):
        g, rest = divmod(row, FIELDS)
        z, f = divmod(rest, 36)
        if f < 32:
            out[row, z * 128 + g * 32 + f] = 1.0
        else:
            out[row, 512 + z * 128 + 4 * g + f - 32 : 512 + (z + 1) * 128 : 16] = 1.0
    return out


def quarter_trig(turns):
    near = jnp.floor(turns + 0.5)
    t = turns - near
    t2 = t * t
    h = math.pi / 2
    sine = t * (h + t2 * (-(h**3) / 6 + t2 * (h**5 / 120 + t2 * (-(h**7) / 5040 + t2 * (h**9 / 362880)))))
    cosine = 1.0 + t2 * (-(h**2) / 2 + t2 * (h**4 / 24 + t2 * (-(h**6) / 720 + t2 * (h**8 / 40320))))
    quadrant = near - 4.0 * jnp.floor(near * 0.25)
    odd = (quadrant == 1.0) | (quadrant == 3.0)
    c = jnp.where(odd, sine, cosine)
    s = jnp.where(odd, cosine, sine)
    c = jnp.where((quadrant == 1.0) | (quadrant == 2.0), -c, c)
    s = jnp.where(quadrant >= 2.0, -s, s)
    return c, s


def nt(a, b):
    return lax.dot_general(a, b, (((1,), (1,)), ((), ())), preferred_element_type=F32)


def exchange(
    rows_ref, lon_ref, wave_ref, inv_ref, leg_hbm, spec_hbm, perm_ref, lhs_hbm, tab_hbm,
    leg, spec, left, north, south, entry, hot, sbuf, rbuf, vmat, lhs, tab,
    load_sem, gs_sem, gr_sem, send_sem, recv_sem, own_sem, out_sem, tab_sem,
):
    here = place()
    me = order_of(*here)

    def load(k):
        part = pl.ds(k * 8, 8)
        return (
            pltpu.make_async_copy(leg_hbm.at[part], leg.at[part], load_sem.at[k, 0]),
            pltpu.make_async_copy(spec_hbm.at[part], spec.at[part], load_sem.at[k, 1]),
        )

    for k in range(CHUNKS):
        for copy in load(k):
            copy.start()

    barrier = pltpu.get_barrier_semaphore()
    for offset in PLANE + LINE:
        pl.semaphore_signal(barrier, inc=1, device_id=neighbour(here, offset)[0], device_id_type=MESH)

    lane = lax.broadcasted_iota(jnp.int32, (1, 128), 1)
    mine = jnp.where(lane == 0, rows_ref[0], jnp.where(lane == 1, rows_ref[1], wave_ref[0] // SLOTS))
    entry[pl.ds(me, 1)] = mine.astype(F32).reshape(1, 1, 128)
    left[...] = jnp.zeros_like(left)
    depth_index = lax.broadcasted_iota(jnp.int32, (1, DEPTH), 1)
    sign = jnp.where(depth_index % 2 == 0, 1.0, -1.0)

    def legendre_part(k):
        for copy in load(k):
            copy.wait()

        def one(s, _):
            used = jnp.where(depth_index < DEPTH - wave_ref[s], 1.0, 0.0)
            values = spec[s]
            left[pl.ds(0, COLS), :] = values * used.astype(BF16)
            left[pl.ds(80, COLS), :] = values * (used * sign).astype(BF16)
            sums = jnp.dot(left[...], leg[s], preferred_element_type=F32)
            at = pl.multiple_of(s * COLS, 8)
            north[pl.ds(at, COLS), :] = sums[:COLS]
            south[pl.ds(at, COLS), :] = sums[80 : 80 + COLS]
            return 0

        lax.fori_loop(k * 8, k * 8 + 8, one, 0)

    def gather(offsets, size, first):
        base = (me // size) * size
        copies = []
        for n, offset in enumerate(offsets):
            block = entry.at[pl.ds(base, size)]
            copies.append(
                pltpu.make_async_remote_copy(
                    src_ref=block, dst_ref=block, send_sem=gs_sem.at[first + n], recv_sem=gr_sem.at[first + n],
                    device_id=neighbour(here, offset)[0], device_id_type=MESH,
                )
            )
        return copies

    legendre_part(0)
    legendre_part(1)
    pl.semaphore_wait(barrier, len(PLANE) + len(LINE))
    plane = gather(PLANE, 1, 0)
    for copy in plane:
        copy.start()
    legendre_part(2)
    legendre_part(3)
    for copy in plane:
        copy.wait()
    line = gather(LINE, 16, len(PLANE))
    for copy in line:
        copy.start()
    legendre_part(4)
    for copy in line:
        copy.wait()

    known = entry[...].reshape(PEERS, 128)
    lat = lax.broadcasted_iota(jnp.int32, (PEERS, 256), 1).astype(F32)
    for r in range(2):
        hot[r] = jnp.where(known[:, r : r + 1] == lat, 1.0, 0.0).astype(BF16)
    runs = jnp.concatenate([known[0:16, 2:3], known[64:80, 2:3]], axis=0)

    def send(e, _):
        tails = []
        for c in range(2):
            for u in range(2):
                main, tail = [], []
                for g in range(4):
                    at = inv_ref[(e * 2 + u) * 4 + g] * COLS + c
                    main.append(
                        jnp.concatenate([ref[pl.ds(at, 32, stride=2), :] for ref in (north, south)], axis=1)
                    )
                    tail.append(
                        jnp.concatenate([ref[pl.ds(at + 64, 4, stride=2), :] for ref in (north, south)], axis=1)
                    )
                tails += tail
                main = jnp.concatenate(main, axis=0).astype(BF16)
                for r in range(2):
                    i = r * 4 + c * 2 + u
                    sbuf[pl.ds(e * PEERS * PITCH + i, PEERS, stride=PITCH), :] = nt(hot[r], main)
        tails = jnp.concatenate(tails, axis=0).astype(BF16)
        sbuf[pl.ds(e * PEERS * PITCH + 8, PEERS, stride=PITCH), :] = jnp.concatenate(
            [nt(hot[0], tails), nt(hot[1], tails)], axis=1
        )

        def one(n, _):
            n = lax.rem(n * 53, PEERS)
            device, to = neighbour(here, (n // 32, (n // 8) % 4, (n // 4) % 2, n % 4))
            pltpu.make_async_remote_copy(
                src_ref=sbuf.at[pl.ds((e * PEERS + to) * PITCH, TILES)],
                dst_ref=rbuf.at[pl.ds((e * PEERS + me) * PITCH, TILES)],
                send_sem=send_sem.at[e], recv_sem=recv_sem.at[e], device_id=device, device_id_type=MESH,
            ).start()
            return 0

        lax.fori_loop(1, PEERS, one, 0)
        own = pl.ds((e * PEERS + me) * PITCH, TILES)
        pltpu.make_async_copy(sbuf.at[own], rbuf.at[own], own_sem.at[e]).start()
        return 0

    lax.fori_loop(0, CHUNKS, send, 0)

    column = lax.broadcasted_iota(jnp.int32, (1, 128), 1).astype(F32)

    def fill(n, _):
        r, block = n // (WIDTH // 128), lax.rem(n, WIDTH // 128)
        quarter = (lon_ref[r] // 4).astype(F32)
        inverse = 1.0 / quarter
        p = column + (block * 128).astype(F32)
        at = pl.multiple_of(block * 128, 128)
        for e in range(CHUNKS):
            for u in range(2):
                whole = (runs * 10.0 + (2 * e + u)) * p
                rest = whole - jnp.floor(whole * inverse) * quarter
                c, s = quarter_trig(rest * (4.0 * inverse))
                tab[r, pl.ds(e * 128 + u * 32, 32), pl.ds(at, 128)] = c.astype(BF16)
                tab[r, pl.ds(e * 128 + 64 + u * 32, 32), pl.ds(at, 128)] = s.astype(BF16)
        return 0

    lax.fori_loop(0, 2 * (WIDTH // 128), fill, 0)
    tab_copy = pltpu.make_async_copy(tab, tab_hbm, tab_sem)
    tab_copy.start()

    wide = lax.broadcasted_iota(jnp.int32, (1, 128), 1)
    main_g = (wide // 32).astype(F32)
    tail_g = ((wide % 16) // 4).astype(F32)

    def out_copy(e):
        part = pl.ds(pl.multiple_of(e * 128, 128), 128)
        return pltpu.make_async_copy(lhs.at[:, :, part], lhs_hbm.at[:, :, part], out_sem.at[e])

    def take(e, _):
        total = pl.ds(0, (PEERS - 1) * TILES)
        pltpu.make_async_copy(sbuf.at[total], rbuf.at[total], recv_sem.at[e]).wait()
        own = pl.ds((e * PEERS + me) * PITCH, TILES)
        pltpu.make_async_copy(sbuf.at[own], rbuf.at[own], own_sem.at[e]).wait()

        def rows(core, z, tile):
            return rbuf[pl.ds((e * PEERS + (core * 4 + z) * 16) * PITCH + tile, 16, stride=PITCH), :]

        for r in range(2):
            longs = lon_ref[r].astype(F32)
            for u in range(2):
                m0 = (runs * 10.0 + (2 * e + u).astype(F32)) * 4.0
                m_main, m_tail = m0 + main_g, m0 + tail_g
                weight_main = jnp.where(2.0 * m_main < longs, jnp.where(m_main == 0.0, 1.0, 2.0), 0.0)
                weight_tail = jnp.where(2.0 * m_tail < longs, jnp.where(m_tail == 0.0, 1.0, 2.0), 0.0)
                for c in range(2):
                    i = r * 4 + c * 2 + u
                    picked = jnp.where(wide // 16 == i, weight_tail, 0.0)
                    at = r * 128 + c * 64 + u * 32
                    swapped = r * 128 + (1 - c) * 64 + u * 32
                    for z in range(4):
                        for kind, tile, weight in ((0, i, weight_main), (1, 8, picked)):
                            value = jnp.concatenate([rows(0, z, tile), rows(1, z, tile)], axis=0) * weight
                            lanes = pl.ds((kind * 4 + z) * 128, 128)
                            vmat[0, pl.ds(at, 32), lanes] = (value if c == 0 else -value).astype(BF16)
                            vmat[1, pl.ds(swapped, 32), lanes] = value.astype(BF16)
        part = pl.ds(pl.multiple_of(e * 128, 128), 128)
        real = nt(perm_ref[...], vmat[0]).astype(BF16)
        imag = nt(perm_ref[pl.ds(FIELDS, IM_ROWS), :], vmat[1]).astype(BF16)
        for r in range(2):
            lhs[r, pl.ds(0, RE_ROWS), part] = real[:, r * 128 : (r + 1) * 128]
            lhs[r, pl.ds(RE_ROWS, IM_ROWS), part] = imag[:, r * 128 : (r + 1) * 128]
        out_copy(e).start()
        return 0

    lax.fori_loop(0, CHUNKS, take, 0)

    def finish(e, _):
        total = pl.ds(0, (PEERS - 1) * TILES)
        pltpu.make_async_copy(sbuf.at[total], rbuf.at[total], send_sem.at[e]).wait()
        out_copy(e).wait()
        return 0

    lax.fori_loop(0, CHUNKS, finish, 0)
    tab_copy.wait()


def synthesis(lon_ref, lhs_ref, tab_ref, out_ref, zbuf, parts, line):
    r = pl.program_id(0)
    longs = lon_ref[r]
    quarter = longs // 4
    scale = 4.0 / longs.astype(F32)
    parts[...] = jnp.zeros_like(parts)

    def block(n, _):
        at = pl.multiple_of(n * 256, 256)
        zbuf[...] = jnp.dot(lhs_ref[0], tab_ref[0, :, pl.ds(at, 256)], preferred_element_type=F32)
        p = lax.broadcasted_iota(jnp.int32, (8, 256), 1) + at
        inside = jnp.where(p < quarter, 1.0, 0.0)
        pf = p.astype(F32)
        c1, s1 = quarter_trig(pf * scale)
        c2, s2 = quarter_trig(2.0 * pf * scale)
        c3, s3 = quarter_trig(3.0 * pf * scale)
        c1, s1, c2, s2, c3, s3 = (v * inside for v in (c1, s1, c2, s2, c3, s3))

        def rows(b, _):
            def get(row):
                return zbuf[pl.ds(pl.multiple_of(row + b * 8, 8), 8), :]

            re0, re1, re2, re3 = (get(g * FIELDS) for g in range(4))
            im1, im2, im3 = (get(RE_ROWS + g * FIELDS) for g in range(3))
            a0 = re0 * inside
            a2 = c2 * re2 - s2 * im2
            r1, i1 = c1 * re1 - s1 * im1, c1 * im1 + s1 * re1
            r3, i3 = c3 * re3 - s3 * im3, c3 * im3 + s3 * re3
            plus, minus = a0 + a2, a0 - a2
            across, along = r1 + r3, i1 - i3
            at_rows = pl.ds(pl.multiple_of(b * 8, 8), 8)
            for t, value in enumerate((plus + across, minus - along, plus - across, minus + along)):
                parts[t, at_rows, pl.ds(at, 256)] = value
            return 0

        lax.fori_loop(0, FIELDS // 8, rows, 0)
        return 0

    lax.fori_loop(0, WIDTH // 256, block, 0)

    def place_rows(b, _):
        at_rows = pl.ds(pl.multiple_of(b * 8, 8), 8)
        line[...] = jnp.zeros_like(line)
        for t in range(4):
            start = t * quarter
            moved = pltpu.roll(parts[t, at_rows, :], lax.rem(start, 128), axis=1)
            lanes = pl.ds(pl.multiple_of((start // 128) * 128, 128), WIDTH + 128)
            line[:, lanes] = line[:, lanes] + moved
        out_ref[0, at_rows, :] = line[:, :LONS]
        return 0

    lax.fori_loop(0, FIELDS // 8, place_rows, 0)


def on_device(legendre, spectral, slot_wave, band_rows, lon_count):
    slot = jnp.arange(SLOTS, dtype=jnp.int32)
    within = slot_wave % SLOTS
    inverse = jnp.sum(jnp.where(within[None, :] == slot[:, None], slot[None, :], 0), axis=1)
    perm = jnp.asarray(placement_matrix(), BF16)
    anywhere = pl.BlockSpec(memory_space=pl.ANY)
    smem = pl.BlockSpec(memory_space=pltpu.SMEM)
    dma = pltpu.SemaphoreType.DMA
    n_gather = len(PLANE) + len(LINE)
    lhs, tab = pl.pallas_call(
        exchange,
        out_shape=(
            jax.ShapeDtypeStruct((2, RE_ROWS + IM_ROWS, 640), BF16),
            jax.ShapeDtypeStruct((2, 640, WIDTH), BF16),
        ),
        in_specs=[smem, smem, smem, smem, anywhere, anywhere, pl.BlockSpec(memory_space=pltpu.VMEM)],
        out_specs=(anywhere, anywhere),
        scratch_shapes=[
            pltpu.VMEM((SLOTS, DEPTH, NORTH), BF16),
            pltpu.VMEM((SLOTS, COLS, DEPTH), BF16),
            pltpu.VMEM((160, DEPTH), BF16),
            pltpu.VMEM((SLOTS * COLS, 128), F32),
            pltpu.VMEM((SLOTS * COLS, 128), F32),
            pltpu.VMEM((PEERS, 1, 128), F32),
            pltpu.VMEM((2, PEERS, 256), BF16),
            pltpu.VMEM((CHUNKS * PEERS * PITCH, 128), F32),
            pltpu.VMEM((CHUNKS * PEERS * PITCH, 128), F32),
            pltpu.VMEM((2, 256, 1024), BF16),
            pltpu.VMEM((2, RE_ROWS + IM_ROWS, 640), BF16),
            pltpu.VMEM((2, 640, WIDTH), BF16),
            dma((CHUNKS, 2)),
            dma((n_gather,)),
            dma((n_gather,)),
            dma((CHUNKS,)),
            dma((CHUNKS,)),
            dma((CHUNKS,)),
            dma((CHUNKS,)),
            dma,
        ],
        compiler_params=pltpu.CompilerParams(collective_id=0, has_side_effects=True, vmem_limit_bytes=58 << 20),
    )(band_rows, lon_count, slot_wave, inverse, legendre, jnp.swapaxes(spectral, 1, 2), perm)
    return pl.pallas_call(
        synthesis,
        grid_spec=pltpu.PrefetchScalarGridSpec(
            num_scalar_prefetch=1,
            grid=(2,),
            in_specs=[
                pl.BlockSpec((1, RE_ROWS + IM_ROWS, 640), lambda r, _: (r, 0, 0)),
                pl.BlockSpec((1, 640, WIDTH), lambda r, _: (r, 0, 0)),
            ],
            out_specs=pl.BlockSpec((1, FIELDS, LONS), lambda r, _: (r, 0, 0)),
            scratch_shapes=[
                pltpu.VMEM((RE_ROWS + IM_ROWS, 256), F32),
                pltpu.VMEM((4, FIELDS, WIDTH + 128), F32),
                pltpu.VMEM((8, 5504), F32),
            ],
        ),
        out_shape=jax.ShapeDtypeStruct((2, FIELDS, LONS), F32),
        compiler_params=pltpu.CompilerParams(vmem_limit_bytes=58 << 20),
    )(lon_count, lhs, tab)


def solution(mesh):
    return jax.shard_map(
        on_device,
        mesh=mesh,
        in_specs=(
            P("wave", None, None),
            P("wave", None, "lev"),
            P("wave"),
            P(("wave", "lev")),
            P(("wave", "lev")),
        ),
        out_specs=P(("wave", "lev"), None, None),
        check_vma=False,
    )
```

```python
import functools
import math

import jax
import jax.numpy as jnp
import numpy as np
from jax import lax
from jax.experimental import pallas as pl
from jax.experimental.pallas import tpu as pltpu
from jax.sharding import PartitionSpec as P

MESH = pl.DeviceIdType.MESH
F32 = jnp.float32
BF16 = jnp.bfloat16

SLOTS = 40
DEPTH = 1280
NORTH = 128
COLS = 72
FIELDS = 144
CHUNKS = 5
TILES = 9
GROUPS = (2, 2, 1)
PITCH = 24
PEERS = 128
WIDTH = 1408
HALF = 72
RE_ROWS = 4 * HALF
IM_ROWS = 3 * HALF
ROWS = RE_ROWS + IM_ROWS
TURNS = 56
LONS = 5136


def place():
    wave = lax.axis_index("wave")
    return wave // 8, (wave // 2) % 4, wave % 2, lax.axis_index("lev")


def order_of(y, x, core, z):
    return ((core * 4 + z) * 4 + x) * 4 + y


def neighbour(here, offset):
    y = lax.rem(here[0] + offset[0], 4)
    x = lax.rem(here[1] + offset[1], 4)
    core = lax.rem(here[2] + offset[2], 2)
    z = lax.rem(here[3] + offset[3], 4)
    return ((y * 4 + x) * 2 + core, z), order_of(y, x, core, z)


PLANE = [(y, x, 0, 0) for y in range(4) for x in range(4) if y or x]
LINE_PLACES = [(1, 0), (0, 1), (1, 2), (0, 3), (1, 1), (0, 2), (1, 3)]
LINE = [(0, 0, core, z) for core in range(2) for z in range(4) if core or z]


def placement_matrix():
    out = np.zeros((2, 4, HALF, 1024), np.float32)
    for half in range(2):
        for g in range(4):
            for f in range(HALF):
                z, k = divmod(half * HALF + f, 36)
                if k < 32:
                    out[half, g, f, z * 128 + g * 32 + k] = 1.0
                else:
                    out[half, g, f, 512 + z * 128 + 4 * g + k - 32 : 512 + (z + 1) * 128 : 16] = 1.0
    return out.reshape(2, RE_ROWS, 1024)


def quarter_trig(turns):
    near = jnp.floor(turns + 0.5)
    t = turns - near
    t2 = t * t
    h = math.pi / 2
    sine = t * (h + t2 * (-(h**3) / 6 + t2 * (h**5 / 120 + t2 * (-(h**7) / 5040 + t2 * (h**9 / 362880)))))
    cosine = 1.0 + t2 * (-(h**2) / 2 + t2 * (h**4 / 24 + t2 * (-(h**6) / 720 + t2 * (h**8 / 40320))))
    quadrant = near - 4.0 * jnp.floor(near * 0.25)
    odd = (quadrant == 1.0) | (quadrant == 3.0)
    c = jnp.where(odd, sine, cosine)
    s = jnp.where(odd, cosine, sine)
    c = jnp.where((quadrant == 1.0) | (quadrant == 2.0), -c, c)
    s = jnp.where(quadrant >= 2.0, -s, s)
    return c, s


def nt(a, b):
    return lax.dot_general(a, b, (((1,), (1,)), ((), ())), preferred_element_type=F32)


def exchange(
    rows_ref, lon_ref, wave_ref, leg_hbm, spec_hbm, perm_hbm, lhs_hbm, tab_hbm, turn_hbm,
    leg, spec, perm, left, north, south, entry, inv_vmem, inv_ref, hot, sbuf, rbuf, vmat, lhs, tab, turn,
    load_sem, perm_sem, inv_sem, gs_sem, gr_sem, send_sem, recv_sem, own_sem, out_sem, tab_sem, turn_sem,
):
    here = place()
    me = order_of(*here)

    def load(k):
        part = pl.ds(k * 8, 8)
        return (
            pltpu.make_async_copy(leg_hbm.at[part], leg.at[part], load_sem.at[k, 0]),
            pltpu.make_async_copy(spec_hbm.at[part], spec.at[part], load_sem.at[k, 1]),
        )

    for k in range(CHUNKS):
        for copy in load(k):
            copy.start()

    perm_copy = pltpu.make_async_copy(perm_hbm, perm, perm_sem)
    perm_copy.start()

    barrier = pltpu.get_barrier_semaphore()
    for offset in PLANE + LINE:
        pl.semaphore_signal(barrier, inc=1, device_id=neighbour(here, offset)[0], device_id_type=MESH)

    lane = lax.broadcasted_iota(jnp.int32, (1, 128), 1)
    mine = jnp.where(lane == 0, rows_ref[0], jnp.where(lane == 1, rows_ref[1], wave_ref[0] // SLOTS))
    entry[pl.ds(me, 1)] = mine.astype(F32).reshape(1, 1, 128)
    left[...] = jnp.zeros_like(left)

    within = jnp.full((1, 128), SLOTS, jnp.int32)
    for s in range(SLOTS):
        within = jnp.where(lane == s, lax.rem(wave_ref[s], SLOTS), within)
    wanted = lax.broadcasted_iota(jnp.int32, (SLOTS, 128), 0)
    slot = lax.broadcasted_iota(jnp.int32, (SLOTS, 128), 1)
    found = jnp.max(jnp.where(within == wanted, slot, 0), axis=1, keepdims=True)
    inv_vmem[...] = jnp.broadcast_to(found, (SLOTS, 128))
    inv_copy = pltpu.make_async_copy(inv_vmem, inv_ref, inv_sem)
    inv_copy.start()
    depth_index = lax.broadcasted_iota(jnp.int32, (1, DEPTH), 1)
    sign = jnp.where(depth_index % 2 == 0, 1.0, -1.0)

    def legendre_part(k):
        for copy in load(k):
            copy.wait()

        def four(n, _):
            for q in range(4):
                s = k * 8 + n * 4 + q
                used = jnp.where(depth_index < DEPTH - wave_ref[s], 1.0, 0.0)
                values = spec[s]
                left[q, pl.ds(0, COLS), :] = values * used.astype(BF16)
                left[q, pl.ds(80, COLS), :] = values * (used * sign).astype(BF16)
                sums = jnp.dot(left[q], leg[s], preferred_element_type=F32)
                at = pl.multiple_of(s * COLS, 8)
                north[pl.ds(at, COLS), :] = sums[:COLS]
                south[pl.ds(at, COLS), :] = sums[80 : 80 + COLS]
            return 0

        lax.fori_loop(0, 2, four, 0)

    def gather(offsets, size, first):
        base = (me // size) * size
        copies = []
        for n, offset in enumerate(offsets):
            block = entry.at[pl.ds(base, size)]
            copies.append(
                pltpu.make_async_remote_copy(
                    src_ref=block, dst_ref=block, send_sem=gs_sem.at[first + n], recv_sem=gr_sem.at[first + n],
                    device_id=neighbour(here, offset)[0], device_id_type=MESH,
                )
            )
        return copies

    legendre_part(0)
    legendre_part(1)
    pl.semaphore_wait(barrier, len(PLANE) + len(LINE))
    plane = gather(PLANE, 1, 0)
    for copy in plane:
        copy.start()
    legendre_part(2)
    legendre_part(3)
    for copy in plane:
        copy.wait()
    line = gather(LINE, 16, len(PLANE))
    for copy in line:
        copy.start()
    legendre_part(4)
    for copy in line:
        copy.wait()

    inv_copy.wait()
    perm_copy.wait()
    known = entry[...].reshape(PEERS, 128)
    lat = lax.broadcasted_iota(jnp.int32, (PEERS, 256), 1).astype(F32)
    for r in range(2):
        hot[r] = jnp.where(known[:, r : r + 1] == lat, 1.0, 0.0).astype(BF16)
    runs = jnp.concatenate([known[0:16, 2:3], known[64:80, 2:3]], axis=0)

    def first_row(e):
        return (e // 2) * PEERS * PITCH + (e % 2) * TILES

    def pack(e, _):
        tails = []
        for c in range(2):
            for u in range(2):
                main, tail = [], []
                for g in range(4):
                    at = inv_ref[(e * 2 + u) * 4 + g, 0] * COLS + c
                    main.append(
                        jnp.concatenate([ref[pl.ds(at, 32, stride=2), :] for ref in (north, south)], axis=1)
                    )
                    tail.append(
                        jnp.concatenate([ref[pl.ds(at + 64, 4, stride=2), :] for ref in (north, south)], axis=1)
                    )
                tails += tail
                main = jnp.concatenate(main, axis=0).astype(BF16)
                for r in range(2):
                    i = r * 4 + c * 2 + u
                    sbuf[pl.ds(first_row(e) + i, PEERS, stride=PITCH), :] = nt(hot[r], main)
        tails = jnp.concatenate(tails, axis=0).astype(BF16)
        sbuf[pl.ds(first_row(e) + 8, PEERS, stride=PITCH), :] = jnp.concatenate(
            [nt(hot[0], tails), nt(hot[1], tails)], axis=1
        )

        return 0

    def own_copy(k):
        own = pl.ds((k * PEERS + me) * PITCH, GROUPS[k] * TILES)
        return pltpu.make_async_copy(sbuf.at[own], rbuf.at[own], own_sem.at[k])

    def send(k, n, skip):
        for j, (core, z) in enumerate([(0, 0)] + LINE_PLACES):
            if j == skip:
                continue
            xy = lax.rem(n * 5 + j * 7, 16)
            device, to = neighbour(here, (xy // 4, lax.rem(xy, 4), core, z))
            size = GROUPS[k] * TILES
            pltpu.make_async_remote_copy(
                src_ref=sbuf.at[pl.ds((k * PEERS + to) * PITCH, size)],
                dst_ref=rbuf.at[pl.ds((k * PEERS + me) * PITCH, size)],
                send_sem=send_sem.at[k], recv_sem=recv_sem.at[k], device_id=device, device_id_type=MESH,
            ).start()

    column = lax.broadcasted_iota(jnp.int32, (1, 128), 1).astype(F32)

    def fill(n, _):
        r, block = n // (WIDTH // 128), lax.rem(n, WIDTH // 128)
        quarter = (lon_ref[r] // 4).astype(F32)
        inverse = 1.0 / quarter
        p = column + (block * 128).astype(F32)
        at = pl.multiple_of(block * 128, 128)
        for e in range(CHUNKS):
            for u in range(2):
                whole = (runs * 10.0 + (2 * e + u)) * p
                rest = whole - jnp.floor(whole * inverse) * quarter
                c, s = quarter_trig(rest * (4.0 * inverse))
                tab[r, pl.ds(e * 128 + u * 32, 32), pl.ds(at, 128)] = c.astype(BF16)
                tab[r, pl.ds(e * 128 + 64 + u * 32, 32), pl.ds(at, 128)] = s.astype(BF16)
        step = 4.0 / lon_ref[r].astype(F32)
        inside = jnp.where(p < quarter, 1.0, 0.0)
        kept = [inside]
        for g in range(1, 4):
            kept += quarter_trig(p * (g * step))
        for k, value in enumerate(kept):
            turn[r, pl.ds(k * 8, 8), pl.ds(at, 128)] = jnp.broadcast_to(value * inside, (8, 128))
        return 0

    tab_copy = pltpu.make_async_copy(tab, tab_hbm, tab_sem)
    turn_copy = pltpu.make_async_copy(turn, turn_hbm, turn_sem)

    wide = lax.broadcasted_iota(jnp.int32, (1, 128), 1)
    main_g = (wide // 32).astype(F32)
    tail_g = ((wide % 16) // 4).astype(F32)

    def out_copy(e):
        part = pl.ds(pl.multiple_of(e * 128, 128), 128)
        return pltpu.make_async_copy(lhs.at[:, :, part], lhs_hbm.at[:, :, part], out_sem.at[e])

    def take(e, _):
        def rows(core, z, tile):
            return rbuf[pl.ds(first_row(e) + (core * 4 + z) * 16 * PITCH + tile, 16, stride=PITCH), :]

        for r in range(2):
            longs = lon_ref[r].astype(F32)
            for u in range(2):
                m0 = (runs * 10.0 + (2 * e + u).astype(F32)) * 4.0
                m_main, m_tail = m0 + main_g, m0 + tail_g
                weight_main = jnp.where(2.0 * m_main < longs, jnp.where(m_main == 0.0, 1.0, 2.0), 0.0)
                weight_tail = jnp.where(2.0 * m_tail < longs, jnp.where(m_tail == 0.0, 1.0, 2.0), 0.0)
                for c in range(2):
                    i = r * 4 + c * 2 + u
                    picked = jnp.where(wide // 16 == i, weight_tail, 0.0)
                    at = r * 128 + c * 64 + u * 32
                    swapped = r * 128 + (1 - c) * 64 + u * 32
                    for z in range(4):
                        for kind, tile, weight in ((0, i, weight_main), (1, 8, picked)):
                            value = jnp.concatenate([rows(0, z, tile), rows(1, z, tile)], axis=0) * weight
                            lanes = pl.ds((kind * 4 + z) * 128, 128)
                            vmat[0, pl.ds(at, 32), lanes] = (value if c == 0 else -value).astype(BF16)
                            vmat[1, pl.ds(swapped, 32), lanes] = value.astype(BF16)
        part = pl.ds(pl.multiple_of(e * 128, 128), 128)
        for half in range(2):
            real = nt(perm[half], vmat[0]).astype(BF16)
            imag = nt(perm[half, pl.ds(HALF, IM_ROWS), :], vmat[1]).astype(BF16)
            for r in range(2):
                lhs[r * 2 + half, pl.ds(0, RE_ROWS), part] = real[:, r * 128 : (r + 1) * 128]
                lhs[r * 2 + half, pl.ds(RE_ROWS, IM_ROWS), part] = imag[:, r * 128 : (r + 1) * 128]
        out_copy(e).start()
        return 0

    def whole(k, sem):
        total = pl.ds(0, (PEERS - 1) * GROUPS[k] * TILES)
        return pltpu.make_async_copy(sbuf.at[total], rbuf.at[total], sem.at[k])

    blocks = 2 * (WIDTH // 128)
    done = 0
    for k in range(3):
        lax.fori_loop(2 * k, 2 * k + GROUPS[k], pack, 0)
        own_copy(k).start()
        send(k, 0, 0)
        filled = min(done + 15, blocks)

        def some(n, _):
            send(k, n, -1)
            fill(done + n - 1, 0)
            return 0

        def rest(n, _):
            send(k, n, -1)
            return 0

        lax.fori_loop(1, 1 + filled - done, some, 0)
        lax.fori_loop(1 + filled - done, 16, rest, 0)
        done = filled
    tab_copy.start()
    turn_copy.start()
    for k in range(3):
        whole(k, recv_sem).wait()
        own_copy(k).wait()
        lax.fori_loop(2 * k, 2 * k + GROUPS[k], take, 0)
    for k in range(3):
        whole(k, send_sem).wait()
    for e in range(CHUNKS):
        out_copy(e).wait()
    tab_copy.wait()
    turn_copy.wait()


def synthesis(
    lon_ref, lhs_hbm, tab_hbm, turn_hbm, out_hbm,
    lhs, tab, turn, z0, z1, parts0, parts1, out0, out1, lhs_sem, tab_sem, turn_sem, out_sem,
):
    sums, outs = (z0, z1), (out0, out1)

    def lhs_copy(s):
        return pltpu.make_async_copy(lhs_hbm.at[s], lhs.at[s], lhs_sem.at[s])

    def tab_copy(r):
        return pltpu.make_async_copy(tab_hbm.at[r], tab.at[r], tab_sem.at[r])

    def turn_copy(r):
        return pltpu.make_async_copy(turn_hbm.at[r], turn.at[r], turn_sem.at[r])

    def out_copy(s):
        rows = out_hbm.at[s // 2, pl.ds((s % 2) * HALF, HALF), :]
        return pltpu.make_async_copy(outs[s % 2], rows, out_sem.at[s % 2])

    tab_copy(0).start()
    lhs_copy(0).start()
    turn_copy(0).start()
    lhs_copy(1).start()
    tab_copy(1).start()
    turn_copy(1).start()
    lhs_copy(2).start()
    lhs_copy(3).start()
    for ref in sums:
        ref[:, WIDTH - 128 :] = jnp.zeros((ROWS, 128), F32)
    lane = lax.broadcasted_iota(jnp.int32, (8, 128), 1)

    def product(s, at, width):
        sums[s % 2][:, pl.ds(at, width)] = jnp.dot(
            lhs[s], tab[s // 2, :, pl.ds(at, width)], preferred_element_type=F32
        )

    def unit(s, b, parts):
        source, out, r = sums[s % 2], outs[s % 2], s // 2
        quarter = lon_ref[r] // 4
        rows = pl.ds(pl.multiple_of(b * 8, 8), 8)
        for j in range(WIDTH // 128):
            lanes = pl.ds(j * 128, 128)

            def get(row):
                return source[pl.ds(pl.multiple_of(row * HALF + b * 8, 8), 8), lanes]

            re0, re1, re2, re3, im1, im2, im3 = (get(k) for k in range(7))
            inside, c1, s1, c2, s2, c3, s3 = (turn[r, pl.ds(k * 8, 8), lanes] for k in range(7))
            a0 = re0 * inside
            a2 = c2 * re2 - s2 * im2
            r1, i1 = c1 * re1 - s1 * im1, c1 * im1 + s1 * re1
            r3, i3 = c3 * re3 - s3 * im3, c3 * im3 + s3 * re3
            plus, minus = a0 + a2, a0 - a2
            across, along = r1 + r3, i1 - i3
            for t, value in enumerate((plus + across, minus - along, plus - across, minus + along)):
                parts[pl.ds(t * 8, 8), lanes] = value
        for t in range(4):
            start = t * quarter
            first, shift = start // 128, lax.rem(start, 128)
            below = lane < shift
            before = out[rows, pl.ds(pl.multiple_of(first * 128, 128), 128)]
            previous = None
            for j in range(WIDTH // 128):
                turned = pltpu.roll(parts[pl.ds(t * 8, 8), pl.ds(j * 128, 128)], shift, axis=1)
                value = jnp.where(below, before, turned)
                before = turned
                if t == 3 and j == WIDTH // 128 - 1:
                    full = first == 30
                    out[rows, pl.ds(5120, 16)] = jnp.where(full, value, 0.0)[:, :16]
                    value = jnp.where(full, previous, value)
                    place_at = jnp.minimum(first + j, 39)
                else:
                    place_at = first + j
                out[rows, pl.ds(pl.multiple_of(place_at * 128, 128), 128)] = value
                previous = value

    for s in range(5):
        if s < 4:
            lhs_copy(s).wait()
            if s % 2 == 0:
                tab_copy(s // 2).wait()
        if s >= 1:
            if s % 2 == 1:
                turn_copy(s // 2).wait()
            if s >= 3:
                out_copy(s - 3).wait()
            out = outs[(s - 1) % 2]
            covered = (3 * (lon_ref[(s - 1) // 2] // 4)) // 128 + 11

            def clear(tile, _):
                out[:, pl.ds(pl.multiple_of(tile * 128, 128), 128)] = jnp.zeros((HALF, 128), F32)
                return 0

            lax.fori_loop(covered, 40, clear, 0)

        def block(n, _):
            if s < 4:
                product(s, pl.multiple_of(n * 256, 256), 256)
            if s >= 1:
                unit(s - 1, n * 2, parts0)
                unit(s - 1, jnp.minimum(n * 2 + 1, HALF // 8 - 1), parts1)
            return 0

        lax.fori_loop(0, 5, block, 0)
        if s < 4:

            @pl.when(lon_ref[s // 2] > 5120)
            def _():
                product(s, 1280, 128)

        if s >= 1:
            out_copy(s - 1).start()
    out_copy(2).wait()
    out_copy(3).wait()


def on_device(legendre, spectral, slot_wave, band_rows, lon_count):
    perm = jnp.asarray(placement_matrix(), BF16)
    anywhere = pl.BlockSpec(memory_space=pl.ANY)
    smem = pl.BlockSpec(memory_space=pltpu.SMEM)
    dma = pltpu.SemaphoreType.DMA
    n_gather = len(PLANE) + len(LINE)
    lhs, tab, turn = pl.pallas_call(
        exchange,
        out_shape=(
            jax.ShapeDtypeStruct((4, ROWS, 640), BF16),
            jax.ShapeDtypeStruct((2, 640, WIDTH), BF16),
            jax.ShapeDtypeStruct((2, TURNS, WIDTH), F32),
        ),
        in_specs=[smem, smem, smem, anywhere, anywhere, anywhere],
        out_specs=(anywhere, anywhere, anywhere),
        scratch_shapes=[
            pltpu.VMEM((SLOTS, DEPTH, NORTH), BF16),
            pltpu.VMEM((SLOTS, COLS, DEPTH), BF16),
            pltpu.VMEM((2, RE_ROWS, 1024), BF16),
            pltpu.VMEM((4, 160, DEPTH), BF16),
            pltpu.VMEM((SLOTS * COLS, 128), F32),
            pltpu.VMEM((SLOTS * COLS, 128), F32),
            pltpu.VMEM((PEERS, 1, 128), F32),
            pltpu.VMEM((SLOTS, 128), jnp.int32),
            pltpu.SMEM((SLOTS, 128), jnp.int32),
            pltpu.VMEM((2, PEERS, 256), BF16),
            pltpu.VMEM((len(GROUPS) * PEERS * PITCH, 128), F32),
            pltpu.VMEM((len(GROUPS) * PEERS * PITCH, 128), F32),
            pltpu.VMEM((2, 256, 1024), BF16),
            pltpu.VMEM((4, ROWS, 640), BF16),
            pltpu.VMEM((2, 640, WIDTH), BF16),
            pltpu.VMEM((2, TURNS, WIDTH), F32),
            dma((CHUNKS, 2)),
            dma,
            dma,
            dma((n_gather,)),
            dma((n_gather,)),
            dma((len(GROUPS),)),
            dma((len(GROUPS),)),
            dma((len(GROUPS),)),
            dma((CHUNKS,)),
            dma,
            dma,
        ],
        compiler_params=pltpu.CompilerParams(collective_id=0, has_side_effects=True, vmem_limit_bytes=58 << 20),
    )(band_rows, lon_count, slot_wave, legendre, jnp.swapaxes(spectral, 1, 2), perm)
    return pl.pallas_call(
        synthesis,
        out_shape=jax.ShapeDtypeStruct((2, FIELDS, LONS), F32),
        in_specs=[smem, anywhere, anywhere, anywhere],
        out_specs=anywhere,
        scratch_shapes=[
            pltpu.VMEM((4, ROWS, 640), BF16),
            pltpu.VMEM((2, 640, WIDTH), BF16),
            pltpu.VMEM((2, TURNS, WIDTH), F32),
            pltpu.VMEM((ROWS, WIDTH), F32),
            pltpu.VMEM((ROWS, WIDTH), F32),
            pltpu.VMEM((32, WIDTH), F32),
            pltpu.VMEM((32, WIDTH), F32),
            pltpu.VMEM((HALF, LONS), F32),
            pltpu.VMEM((HALF, LONS), F32),
            dma((4,)),
            dma((2,)),
            dma((2,)),
            dma((2,)),
        ],
        compiler_params=pltpu.CompilerParams(vmem_limit_bytes=58 << 20),
    )(lon_count, lhs, tab, turn)


def solution(mesh):
    return jax.shard_map(
        on_device,
        mesh=mesh,
        in_specs=(
            P("wave", None, None),
            P("wave", None, "lev"),
            P("wave"),
            P(("wave", "lev")),
            P(("wave", "lev")),
        ),
        out_specs=P(("wave", "lev"), None, None),
        check_vma=False,
    )
```

```python
import functools
import math

import jax
import jax.numpy as jnp
import numpy as np
from jax import lax
from jax.experimental import pallas as pl
from jax.experimental.pallas import tpu as pltpu
from jax.sharding import PartitionSpec as P

MESH = pl.DeviceIdType.MESH
F32 = jnp.float32
BF16 = jnp.bfloat16

SLOTS = 40
DEPTH = 1280
NORTH = 128
COLS = 72
FIELDS = 144
CHUNKS = 5
TILES = 9
GROUPS = (2, 2, 1)
PITCH = 24
PEERS = 128
WIDTH = 1408
HALF = 72
RE_ROWS = 4 * HALF
IM_ROWS = 3 * HALF
ROWS = RE_ROWS + IM_ROWS
TURNS = 56
LONS = 5136


def place():
    wave = lax.axis_index("wave")
    return wave // 8, (wave // 2) % 4, wave % 2, lax.axis_index("lev")


def order_of(y, x, core, z):
    return ((core * 4 + z) * 4 + x) * 4 + y


def neighbour(here, offset):
    y = lax.rem(here[0] + offset[0], 4)
    x = lax.rem(here[1] + offset[1], 4)
    core = lax.rem(here[2] + offset[2], 2)
    z = lax.rem(here[3] + offset[3], 4)
    return ((y * 4 + x) * 2 + core, z), order_of(y, x, core, z)


PLANE = [(y, x, 0, 0) for y in range(4) for x in range(4) if y or x]
LINE_PLACES = [(1, 0), (0, 1), (1, 2), (0, 3), (1, 1), (0, 2), (1, 3)]
LINE = [(0, 0, core, z) for core in range(2) for z in range(4) if core or z]


def placement_matrix():
    out = np.zeros((2, 4, HALF, 1024), np.float32)
    for half in range(2):
        for g in range(4):
            for f in range(HALF):
                z, k = divmod(half * HALF + f, 36)
                if k < 32:
                    out[half, g, f, z * 128 + g * 32 + k] = 1.0
                else:
                    out[half, g, f, 512 + z * 128 + 4 * g + k - 32 : 512 + (z + 1) * 128 : 16] = 1.0
    return out.reshape(2, RE_ROWS, 1024)


def quarter_trig(turns):
    near = jnp.floor(turns + 0.5)
    t = turns - near
    t2 = t * t
    h = math.pi / 2
    sine = t * (h + t2 * (-(h**3) / 6 + t2 * (h**5 / 120 + t2 * (-(h**7) / 5040 + t2 * (h**9 / 362880)))))
    cosine = 1.0 + t2 * (-(h**2) / 2 + t2 * (h**4 / 24 + t2 * (-(h**6) / 720 + t2 * (h**8 / 40320))))
    quadrant = near - 4.0 * jnp.floor(near * 0.25)
    odd = (quadrant == 1.0) | (quadrant == 3.0)
    c = jnp.where(odd, sine, cosine)
    s = jnp.where(odd, cosine, sine)
    c = jnp.where((quadrant == 1.0) | (quadrant == 2.0), -c, c)
    s = jnp.where(quadrant >= 2.0, -s, s)
    return c, s


def nt(a, b):
    return lax.dot_general(a, b, (((1,), (1,)), ((), ())), preferred_element_type=F32)


def exchange(
    rows_ref, lon_ref, wave_ref, leg_hbm, spec_hbm, perm_hbm, lhs_hbm, tab_hbm, turn_hbm,
    leg, spec, perm, left, north, south, entry, inv_vmem, inv_ref, hot, sbuf, rbuf, vmat, lhs, tab, turn,
    load_sem, perm_sem, inv_sem, gs_sem, gr_sem, send_sem, recv_sem, own_sem, out_sem, tab_sem, turn_sem,
):
    here = place()
    me = order_of(*here)

    def load(k):
        part = pl.ds(k * 8, 8)
        return (
            pltpu.make_async_copy(leg_hbm.at[part], leg.at[part], load_sem.at[k, 0]),
            pltpu.make_async_copy(spec_hbm.at[part], spec.at[part], load_sem.at[k, 1]),
        )

    for k in range(CHUNKS):
        for copy in load(k):
            copy.start()

    perm_copy = pltpu.make_async_copy(perm_hbm, perm, perm_sem)
    perm_copy.start()

    barrier = pltpu.get_barrier_semaphore()
    for offset in PLANE + LINE:
        pl.semaphore_signal(barrier, inc=1, device_id=neighbour(here, offset)[0], device_id_type=MESH)

    lane = lax.broadcasted_iota(jnp.int32, (1, 128), 1)
    mine = jnp.where(lane == 0, rows_ref[0], jnp.where(lane == 1, rows_ref[1], wave_ref[0] // SLOTS))
    entry[pl.ds(me, 1)] = mine.astype(F32).reshape(1, 1, 128)
    left[...] = jnp.zeros_like(left)

    within = jnp.full((1, 128), SLOTS, jnp.int32)
    for s in range(SLOTS):
        within = jnp.where(lane == s, lax.rem(wave_ref[s], SLOTS), within)
    wanted = lax.broadcasted_iota(jnp.int32, (SLOTS, 128), 0)
    slot = lax.broadcasted_iota(jnp.int32, (SLOTS, 128), 1)
    found = jnp.max(jnp.where(within == wanted, slot, 0), axis=1, keepdims=True)
    inv_vmem[...] = jnp.broadcast_to(found, (SLOTS, 128))
    inv_copy = pltpu.make_async_copy(inv_vmem, inv_ref, inv_sem)
    inv_copy.start()
    depth_index = lax.broadcasted_iota(jnp.int32, (1, DEPTH), 1)
    sign = jnp.where(depth_index % 2 == 0, 1.0, -1.0)

    def legendre_part(k):
        for copy in load(k):
            copy.wait()

        def four(n, _):
            for q in range(4):
                s = k * 8 + n * 4 + q
                used = jnp.where(depth_index < DEPTH - wave_ref[s], 1.0, 0.0)
                values = spec[s]
                left[q, pl.ds(0, COLS), :] = values * used.astype(BF16)
                left[q, pl.ds(80, COLS), :] = values * (used * sign).astype(BF16)
                sums = jnp.dot(left[q], leg[s], preferred_element_type=F32)
                at = pl.multiple_of(s * COLS, 8)
                north[pl.ds(at, COLS), :] = sums[:COLS]
                south[pl.ds(at, COLS), :] = sums[80 : 80 + COLS]
            return 0

        lax.fori_loop(0, 2, four, 0)

    def gather(offsets, size, first):
        base = (me // size) * size
        copies = []
        for n, offset in enumerate(offsets):
            block = entry.at[pl.ds(base, size)]
            copies.append(
                pltpu.make_async_remote_copy(
                    src_ref=block, dst_ref=block, send_sem=gs_sem.at[first + n], recv_sem=gr_sem.at[first + n],
                    device_id=neighbour(here, offset)[0], device_id_type=MESH,
                )
            )
        return copies

    legendre_part(0)
    legendre_part(1)
    pl.semaphore_wait(barrier, len(PLANE) + len(LINE))
    plane = gather(PLANE, 1, 0)
    for copy in plane:
        copy.start()
    legendre_part(2)
    legendre_part(3)
    for copy in plane:
        copy.wait()
    line = gather(LINE, 16, len(PLANE))
    for copy in line:
        copy.start()
    legendre_part(4)
    for copy in line:
        copy.wait()

    inv_copy.wait()
    perm_copy.wait()
    known = entry[...].reshape(PEERS, 128)
    lat = lax.broadcasted_iota(jnp.int32, (PEERS, 256), 1).astype(F32)
    for r in range(2):
        hot[r] = jnp.where(known[:, r : r + 1] == lat, 1.0, 0.0).astype(BF16)
    runs = jnp.concatenate([known[0:16, 2:3], known[64:80, 2:3]], axis=0)

    def first_row(e):
        return (e // 2) * PEERS * PITCH + (e % 2) * TILES

    def pack(e, _):
        tails = []
        for c in range(2):
            for u in range(2):
                main, tail = [], []
                for g in range(4):
                    at = inv_ref[(e * 2 + u) * 4 + g, 0] * COLS + c
                    main.append(
                        jnp.concatenate([ref[pl.ds(at, 32, stride=2), :] for ref in (north, south)], axis=1)
                    )
                    tail.append(
                        jnp.concatenate([ref[pl.ds(at + 64, 4, stride=2), :] for ref in (north, south)], axis=1)
                    )
                tails += tail
                main = jnp.concatenate(main, axis=0).astype(BF16)
                for r in range(2):
                    i = r * 4 + c * 2 + u
                    sbuf[pl.ds(first_row(e) + i, PEERS, stride=PITCH), :] = nt(hot[r], main)
        tails = jnp.concatenate(tails, axis=0).astype(BF16)
        sbuf[pl.ds(first_row(e) + 8, PEERS, stride=PITCH), :] = jnp.concatenate(
            [nt(hot[0], tails), nt(hot[1], tails)], axis=1
        )

        return 0

    def own_copy(k):
        own = pl.ds((k * PEERS + me) * PITCH, GROUPS[k] * TILES)
        return pltpu.make_async_copy(sbuf.at[own], rbuf.at[own], own_sem.at[k])

    def send(k, n, skip):
        for j, (core, z) in enumerate([(0, 0)] + LINE_PLACES):
            if j == skip:
                continue
            xy = lax.rem(n * 5 + j * 7, 16)
            device, to = neighbour(here, (xy // 4, lax.rem(xy, 4), core, z))
            size = GROUPS[k] * TILES
            pltpu.make_async_remote_copy(
                src_ref=sbuf.at[pl.ds((k * PEERS + to) * PITCH, size)],
                dst_ref=rbuf.at[pl.ds((k * PEERS + me) * PITCH, size)],
                send_sem=send_sem.at[k], recv_sem=recv_sem.at[k], device_id=device, device_id_type=MESH,
            ).start()

    column = lax.broadcasted_iota(jnp.int32, (1, 128), 1).astype(F32)

    def fill(n, _):
        r, block = n // (WIDTH // 128), lax.rem(n, WIDTH // 128)
        quarter = (lon_ref[r] // 4).astype(F32)
        inverse = 1.0 / quarter
        p = column + (block * 128).astype(F32)
        at = pl.multiple_of(block * 128, 128)
        for e in range(CHUNKS):
            for u in range(2):
                whole = (runs * 10.0 + (2 * e + u)) * p
                rest = whole - jnp.floor(whole * inverse) * quarter
                c, s = quarter_trig(rest * (4.0 * inverse))
                tab[r, pl.ds(e * 128 + u * 32, 32), pl.ds(at, 128)] = c.astype(BF16)
                tab[r, pl.ds(e * 128 + 64 + u * 32, 32), pl.ds(at, 128)] = s.astype(BF16)
        step = 4.0 / lon_ref[r].astype(F32)
        inside = jnp.where(p < quarter, 1.0, 0.0)
        kept = [inside]
        for g in range(1, 4):
            kept += quarter_trig(p * (g * step))
        for k, value in enumerate(kept):
            turn[r, pl.ds(k * 8, 8), pl.ds(at, 128)] = jnp.broadcast_to(value * inside, (8, 128))
        return 0

    tab_copy = pltpu.make_async_copy(tab, tab_hbm, tab_sem)
    turn_copy = pltpu.make_async_copy(turn, turn_hbm, turn_sem)

    wide = lax.broadcasted_iota(jnp.int32, (1, 128), 1)
    main_g = (wide // 32).astype(F32)
    tail_g = ((wide % 16) // 4).astype(F32)

    def out_copy(e):
        part = pl.ds(pl.multiple_of(e * 128, 128), 128)
        return pltpu.make_async_copy(lhs.at[:, :, part], lhs_hbm.at[:, :, part], out_sem.at[e])

    def take(e, _):
        def rows(core, z, tile):
            return rbuf[pl.ds(first_row(e) + (core * 4 + z) * 16 * PITCH + tile, 16, stride=PITCH), :]

        for r in range(2):
            longs = lon_ref[r].astype(F32)
            for u in range(2):
                m0 = (runs * 10.0 + (2 * e + u).astype(F32)) * 4.0
                m_main, m_tail = m0 + main_g, m0 + tail_g
                weight_main = jnp.where(2.0 * m_main < longs, jnp.where(m_main == 0.0, 1.0, 2.0), 0.0)
                weight_tail = jnp.where(2.0 * m_tail < longs, jnp.where(m_tail == 0.0, 1.0, 2.0), 0.0)
                for c in range(2):
                    i = r * 4 + c * 2 + u
                    picked = jnp.where(wide // 16 == i, weight_tail, 0.0)
                    at = r * 128 + c * 64 + u * 32
                    swapped = r * 128 + (1 - c) * 64 + u * 32
                    for z in range(4):
                        for kind, tile, weight in ((0, i, weight_main), (1, 8, picked)):
                            value = jnp.concatenate([rows(0, z, tile), rows(1, z, tile)], axis=0) * weight
                            lanes = pl.ds((kind * 4 + z) * 128, 128)
                            vmat[0, pl.ds(at, 32), lanes] = (value if c == 0 else -value).astype(BF16)
                            vmat[1, pl.ds(swapped, 32), lanes] = value.astype(BF16)
        part = pl.ds(pl.multiple_of(e * 128, 128), 128)
        for half in range(2):
            real = nt(perm[half], vmat[0]).astype(BF16)
            imag = nt(perm[half, pl.ds(HALF, IM_ROWS), :], vmat[1]).astype(BF16)
            for r in range(2):
                lhs[r * 2 + half, pl.ds(0, RE_ROWS), part] = real[:, r * 128 : (r + 1) * 128]
                lhs[r * 2 + half, pl.ds(RE_ROWS, IM_ROWS), part] = imag[:, r * 128 : (r + 1) * 128]
        out_copy(e).start()
        return 0

    def whole(k, sem):
        total = pl.ds(0, (PEERS - 1) * GROUPS[k] * TILES)
        return pltpu.make_async_copy(sbuf.at[total], rbuf.at[total], sem.at[k])

    blocks = 2 * (WIDTH // 128)
    done = 0
    for k in range(3):
        lax.fori_loop(2 * k, 2 * k + GROUPS[k], pack, 0)
        own_copy(k).start()
        send(k, 0, 0)
        filled = min(done + 15, blocks)

        def some(n, _):
            send(k, n, -1)
            fill(done + n - 1, 0)
            return 0

        def rest(n, _):
            send(k, n, -1)
            return 0

        lax.fori_loop(1, 1 + filled - done, some, 0)
        lax.fori_loop(1 + filled - done, 16, rest, 0)
        done = filled
    tab_copy.start()
    turn_copy.start()
    for k in range(3):
        whole(k, recv_sem).wait()
        own_copy(k).wait()
        lax.fori_loop(2 * k, 2 * k + GROUPS[k], take, 0)
    for k in range(3):
        whole(k, send_sem).wait()
    for e in range(CHUNKS):
        out_copy(e).wait()
    tab_copy.wait()
    turn_copy.wait()


def synthesis(
    lon_ref, lhs_hbm, tab_hbm, turn_hbm, out_hbm,
    lhs, tab, turn, z0, z1, parts0, parts1, out0, out1, lhs_sem, tab_sem, turn_sem, out_sem,
):
    sums, outs = (z0, z1), (out0, out1)

    def lhs_copy(s):
        return pltpu.make_async_copy(lhs_hbm.at[s], lhs.at[s], lhs_sem.at[s])

    def tab_copy(r):
        return pltpu.make_async_copy(tab_hbm.at[r], tab.at[r], tab_sem.at[r])

    def turn_copy(r):
        return pltpu.make_async_copy(turn_hbm.at[r], turn.at[r], turn_sem.at[r])

    def out_copy(s):
        rows = out_hbm.at[s // 2, pl.ds((s % 2) * HALF, HALF), :]
        return pltpu.make_async_copy(outs[s % 2], rows, out_sem.at[s % 2])

    tab_copy(0).start()
    lhs_copy(0).start()
    turn_copy(0).start()
    lhs_copy(1).start()
    tab_copy(1).start()
    turn_copy(1).start()
    lhs_copy(2).start()
    lhs_copy(3).start()
    for ref in sums:
        ref[:, WIDTH - 128 :] = jnp.zeros((ROWS, 128), F32)
    lane = lax.broadcasted_iota(jnp.int32, (8, 128), 1)

    def product(s, at, width):
        sums[s % 2][:, pl.ds(at, width)] = jnp.dot(
            lhs[s], tab[s // 2, :, pl.ds(at, width)], preferred_element_type=F32
        )

    def unit(s, b, parts):
        source, out, r = sums[s % 2], outs[s % 2], s // 2
        quarter = lon_ref[r] // 4
        rows = pl.ds(pl.multiple_of(b * 8, 8), 8)
        for j in range(WIDTH // 128):
            lanes = pl.ds(j * 128, 128)

            def get(row):
                return source[pl.ds(pl.multiple_of(row * HALF + b * 8, 8), 8), lanes]

            re0, re1, re2, re3, im1, im2, im3 = (get(k) for k in range(7))
            inside, c1, s1, c2, s2, c3, s3 = (turn[r, pl.ds(k * 8, 8), lanes] for k in range(7))
            a0 = re0 * inside
            a2 = c2 * re2 - s2 * im2
            r1, i1 = c1 * re1 - s1 * im1, c1 * im1 + s1 * re1
            r3, i3 = c3 * re3 - s3 * im3, c3 * im3 + s3 * re3
            plus, minus = a0 + a2, a0 - a2
            across, along = r1 + r3, i1 - i3
            for t, value in enumerate((plus + across, minus - along, plus - across, minus + along)):
                parts[pl.ds(t * 8, 8), lanes] = value
        for t in range(4):
            start = t * quarter
            first, shift = start // 128, lax.rem(start, 128)
            below = lane < shift
            before = out[rows, pl.ds(pl.multiple_of(first * 128, 128), 128)]
            previous = None
            for j in range(WIDTH // 128):
                turned = pltpu.roll(parts[pl.ds(t * 8, 8), pl.ds(j * 128, 128)], shift, axis=1)
                value = jnp.where(below, before, turned)
                before = turned
                if t == 3 and j == WIDTH // 128 - 1:
                    full = first == 30
                    out[rows, pl.ds(5120, 16)] = jnp.where(full, value, 0.0)[:, :16]
                    value = jnp.where(full, previous, value)
                    place_at = jnp.minimum(first + j, 39)
                else:
                    place_at = first + j
                out[rows, pl.ds(pl.multiple_of(place_at * 128, 128), 128)] = value
                previous = value

    for s in range(5):
        if s < 4:
            lhs_copy(s).wait()
            if s % 2 == 0:
                tab_copy(s // 2).wait()
        if s >= 1:
            if s % 2 == 1:
                turn_copy(s // 2).wait()
            if s >= 3:
                out_copy(s - 3).wait()
            out = outs[(s - 1) % 2]
            covered = (3 * (lon_ref[(s - 1) // 2] // 4)) // 128 + 11

            def clear(tile, _):
                out[:, pl.ds(pl.multiple_of(tile * 128, 128), 128)] = jnp.zeros((HALF, 128), F32)
                return 0

            lax.fori_loop(covered, 40, clear, 0)

        if s < 4:
            product(s, 0, 1280)
        if s >= 1:
            for b in range(HALF // 8):
                unit(s - 1, b, (parts0, parts1)[b % 2])
        if s < 4:

            @pl.when(lon_ref[s // 2] > 5120)
            def _():
                product(s, 1280, 128)

        if s >= 1:
            out_copy(s - 1).start()
    out_copy(2).wait()
    out_copy(3).wait()


def on_device(legendre, spectral, slot_wave, band_rows, lon_count):
    perm = jnp.asarray(placement_matrix(), BF16)
    anywhere = pl.BlockSpec(memory_space=pl.ANY)
    smem = pl.BlockSpec(memory_space=pltpu.SMEM)
    dma = pltpu.SemaphoreType.DMA
    n_gather = len(PLANE) + len(LINE)
    lhs, tab, turn = pl.pallas_call(
        exchange,
        out_shape=(
            jax.ShapeDtypeStruct((4, ROWS, 640), BF16),
            jax.ShapeDtypeStruct((2, 640, WIDTH), BF16),
            jax.ShapeDtypeStruct((2, TURNS, WIDTH), F32),
        ),
        in_specs=[smem, smem, smem, anywhere, anywhere, anywhere],
        out_specs=(anywhere, anywhere, anywhere),
        scratch_shapes=[
            pltpu.VMEM((SLOTS, DEPTH, NORTH), BF16),
            pltpu.VMEM((SLOTS, COLS, DEPTH), BF16),
            pltpu.VMEM((2, RE_ROWS, 1024), BF16),
            pltpu.VMEM((4, 160, DEPTH), BF16),
            pltpu.VMEM((SLOTS * COLS, 128), F32),
            pltpu.VMEM((SLOTS * COLS, 128), F32),
            pltpu.VMEM((PEERS, 1, 128), F32),
            pltpu.VMEM((SLOTS, 128), jnp.int32),
            pltpu.SMEM((SLOTS, 128), jnp.int32),
            pltpu.VMEM((2, PEERS, 256), BF16),
            pltpu.VMEM((len(GROUPS) * PEERS * PITCH, 128), F32),
            pltpu.VMEM((len(GROUPS) * PEERS * PITCH, 128), F32),
            pltpu.VMEM((2, 256, 1024), BF16),
            pltpu.VMEM((4, ROWS, 640), BF16),
            pltpu.VMEM((2, 640, WIDTH), BF16),
            pltpu.VMEM((2, TURNS, WIDTH), F32),
            dma((CHUNKS, 2)),
            dma,
            dma,
            dma((n_gather,)),
            dma((n_gather,)),
            dma((len(GROUPS),)),
            dma((len(GROUPS),)),
            dma((len(GROUPS),)),
            dma((CHUNKS,)),
            dma,
            dma,
        ],
        compiler_params=pltpu.CompilerParams(collective_id=0, has_side_effects=True, vmem_limit_bytes=58 << 20),
    )(band_rows, lon_count, slot_wave, legendre, jnp.swapaxes(spectral, 1, 2), perm)
    return pl.pallas_call(
        synthesis,
        out_shape=jax.ShapeDtypeStruct((2, FIELDS, LONS), F32),
        in_specs=[smem, anywhere, anywhere, anywhere],
        out_specs=anywhere,
        scratch_shapes=[
            pltpu.VMEM((4, ROWS, 640), BF16),
            pltpu.VMEM((2, 640, WIDTH), BF16),
            pltpu.VMEM((2, TURNS, WIDTH), F32),
            pltpu.VMEM((ROWS, WIDTH), F32),
            pltpu.VMEM((ROWS, WIDTH), F32),
            pltpu.VMEM((32, WIDTH), F32),
            pltpu.VMEM((32, WIDTH), F32),
            pltpu.VMEM((HALF, LONS), F32),
            pltpu.VMEM((HALF, LONS), F32),
            dma((4,)),
            dma((2,)),
            dma((2,)),
            dma((2,)),
        ],
        compiler_params=pltpu.CompilerParams(vmem_limit_bytes=58 << 20),
    )(lon_count, lhs, tab, turn)


def solution(mesh):
    return jax.shard_map(
        on_device,
        mesh=mesh,
        in_specs=(
            P("wave", None, None),
            P("wave", None, "lev"),
            P("wave"),
            P(("wave", "lev")),
            P(("wave", "lev")),
        ),
        out_specs=P(("wave", "lev"), None, None),
        check_vma=False,
    )
```

```python
import functools
import math

import jax
import jax.numpy as jnp
import numpy as np
from jax import lax
from jax.experimental import pallas as pl
from jax.experimental.pallas import tpu as pltpu
from jax.sharding import PartitionSpec as P

MESH = pl.DeviceIdType.MESH
F32 = jnp.float32
BF16 = jnp.bfloat16

SLOTS = 40
DEPTH = 1280
NORTH = 128
COLS = 72
FIELDS = 144
CHUNKS = 5
TILES = 9
GROUPS = (2, 2, 1)
PITCH = 24
PEERS = 128
WIDTH = 1408
HALF = 72
RE_ROWS = 4 * HALF
IM_ROWS = 3 * HALF
ROWS = RE_ROWS + IM_ROWS
TURNS = 56
LONS = 5136


def place():
    wave = lax.axis_index("wave")
    return wave // 8, (wave // 2) % 4, wave % 2, lax.axis_index("lev")


def order_of(y, x, core, z):
    return ((core * 4 + z) * 4 + x) * 4 + y


def neighbour(here, offset):
    y = lax.rem(here[0] + offset[0], 4)
    x = lax.rem(here[1] + offset[1], 4)
    core = lax.rem(here[2] + offset[2], 2)
    z = lax.rem(here[3] + offset[3], 4)
    return ((y * 4 + x) * 2 + core, z), order_of(y, x, core, z)


PLANE = [(y, x, 0, 0) for y in range(4) for x in range(4) if y or x]
LINE_PLACES = [(1, 0), (0, 1), (1, 2), (0, 3), (1, 1), (0, 2), (1, 3)]
LINE = [(0, 0, core, z) for core in range(2) for z in range(4) if core or z]


def placement_matrix():
    out = np.zeros((2, 4, HALF, 1024), np.float32)
    for half in range(2):
        for g in range(4):
            for f in range(HALF):
                z, k = divmod(half * HALF + f, 36)
                if k < 32:
                    out[half, g, f, z * 128 + g * 32 + k] = 1.0
                else:
                    out[half, g, f, 512 + z * 128 + 4 * g + k - 32 : 512 + (z + 1) * 128 : 16] = 1.0
    return out.reshape(2, RE_ROWS, 1024)


def quarter_trig(turns):
    near = jnp.floor(turns + 0.5)
    t = turns - near
    t2 = t * t
    h = math.pi / 2
    sine = t * (h + t2 * (-(h**3) / 6 + t2 * (h**5 / 120 + t2 * (-(h**7) / 5040 + t2 * (h**9 / 362880)))))
    cosine = 1.0 + t2 * (-(h**2) / 2 + t2 * (h**4 / 24 + t2 * (-(h**6) / 720 + t2 * (h**8 / 40320))))
    quadrant = near - 4.0 * jnp.floor(near * 0.25)
    odd = (quadrant == 1.0) | (quadrant == 3.0)
    c = jnp.where(odd, sine, cosine)
    s = jnp.where(odd, cosine, sine)
    c = jnp.where((quadrant == 1.0) | (quadrant == 2.0), -c, c)
    s = jnp.where(quadrant >= 2.0, -s, s)
    return c, s


def nt(a, b):
    return lax.dot_general(a, b, (((1,), (1,)), ((), ())), preferred_element_type=F32)


def exchange(
    rows_ref, lon_ref, wave_ref, leg_hbm, spec_hbm, perm_hbm, lhs_hbm, tab_hbm, turn_hbm,
    leg, spec, perm, left, north, south, entry, inv_vmem, inv_ref, hot, sbuf, rbuf, vmat, lhs, tab, turn,
    load_sem, perm_sem, inv_sem, gs_sem, gr_sem, send_sem, recv_sem, own_sem, out_sem, tab_sem, turn_sem,
):
    here = place()
    me = order_of(*here)

    def load(k):
        part = pl.ds(k * 8, 8)
        return (
            pltpu.make_async_copy(leg_hbm.at[part], leg.at[part], load_sem.at[k, 0]),
            pltpu.make_async_copy(spec_hbm.at[part], spec.at[part], load_sem.at[k, 1]),
        )

    for k in range(CHUNKS):
        for copy in load(k):
            copy.start()

    perm_copy = pltpu.make_async_copy(perm_hbm, perm, perm_sem)
    perm_copy.start()

    barrier = pltpu.get_barrier_semaphore()
    for offset in PLANE + LINE:
        pl.semaphore_signal(barrier, inc=1, device_id=neighbour(here, offset)[0], device_id_type=MESH)

    lane = lax.broadcasted_iota(jnp.int32, (1, 128), 1)
    mine = jnp.where(lane == 0, rows_ref[0], jnp.where(lane == 1, rows_ref[1], wave_ref[0] // SLOTS))
    entry[pl.ds(me, 1)] = mine.astype(F32).reshape(1, 1, 128)
    left[...] = jnp.zeros_like(left)

    within = jnp.full((1, 128), SLOTS, jnp.int32)
    for s in range(SLOTS):
        within = jnp.where(lane == s, lax.rem(wave_ref[s], SLOTS), within)
    wanted = lax.broadcasted_iota(jnp.int32, (SLOTS, 128), 0)
    slot = lax.broadcasted_iota(jnp.int32, (SLOTS, 128), 1)
    found = jnp.max(jnp.where(within == wanted, slot, 0), axis=1, keepdims=True)
    inv_vmem[...] = jnp.broadcast_to(found, (SLOTS, 128))
    inv_copy = pltpu.make_async_copy(inv_vmem, inv_ref, inv_sem)
    inv_copy.start()
    depth_index = lax.broadcasted_iota(jnp.int32, (1, DEPTH), 1)
    sign = jnp.where(depth_index % 2 == 0, 1.0, -1.0)

    def legendre_part(k):
        for copy in load(k):
            copy.wait()

        def four(n, _):
            for q in range(4):
                s = k * 8 + n * 4 + q
                used = jnp.where(depth_index < DEPTH - wave_ref[s], 1.0, 0.0)
                values = spec[s]
                left[q, pl.ds(0, COLS), :] = values * used.astype(BF16)
                left[q, pl.ds(80, COLS), :] = values * (used * sign).astype(BF16)
                sums = jnp.dot(left[q], leg[s], preferred_element_type=F32)
                at = pl.multiple_of(s * COLS, 8)
                north[pl.ds(at, COLS), :] = sums[:COLS]
                south[pl.ds(at, COLS), :] = sums[80 : 80 + COLS]
            return 0

        lax.fori_loop(0, 2, four, 0)

    def gather(offsets, size, first):
        base = (me // size) * size
        copies = []
        for n, offset in enumerate(offsets):
            block = entry.at[pl.ds(base, size)]
            copies.append(
                pltpu.make_async_remote_copy(
                    src_ref=block, dst_ref=block, send_sem=gs_sem.at[first + n], recv_sem=gr_sem.at[first + n],
                    device_id=neighbour(here, offset)[0], device_id_type=MESH,
                )
            )
        return copies

    pl.semaphore_wait(barrier, len(PLANE) + len(LINE))
    plane = gather(PLANE, 1, 0)
    for copy in plane:
        copy.start()
    legendre_part(0)
    legendre_part(1)
    legendre_part(2)
    for copy in plane:
        copy.wait()
    line = gather(LINE, 16, len(PLANE))
    for copy in line:
        copy.start()
    legendre_part(3)
    legendre_part(4)
    for copy in line:
        copy.wait()

    inv_copy.wait()
    perm_copy.wait()
    known = entry[...].reshape(PEERS, 128)
    lat = lax.broadcasted_iota(jnp.int32, (PEERS, 256), 1).astype(F32)
    for r in range(2):
        hot[r] = jnp.where(known[:, r : r + 1] == lat, 1.0, 0.0).astype(BF16)
    runs = jnp.concatenate([known[0:16, 2:3], known[64:80, 2:3]], axis=0)

    def first_row(e):
        return (e // 2) * PEERS * PITCH + (e % 2) * TILES

    def pack(e, _):
        tails = []
        for c in range(2):
            for u in range(2):
                main, tail = [], []
                for g in range(4):
                    at = inv_ref[(e * 2 + u) * 4 + g, 0] * COLS + c
                    main.append(
                        jnp.concatenate([ref[pl.ds(at, 32, stride=2), :] for ref in (north, south)], axis=1)
                    )
                    tail.append(
                        jnp.concatenate([ref[pl.ds(at + 64, 4, stride=2), :] for ref in (north, south)], axis=1)
                    )
                tails += tail
                main = jnp.concatenate(main, axis=0).astype(BF16)
                for r in range(2):
                    i = r * 4 + c * 2 + u
                    sbuf[pl.ds(first_row(e) + i, PEERS, stride=PITCH), :] = nt(hot[r], main)
        tails = jnp.concatenate(tails, axis=0).astype(BF16)
        sbuf[pl.ds(first_row(e) + 8, PEERS, stride=PITCH), :] = jnp.concatenate(
            [nt(hot[0], tails), nt(hot[1], tails)], axis=1
        )

        return 0

    def own_copy(k):
        own = pl.ds((k * PEERS + me) * PITCH, GROUPS[k] * TILES)
        return pltpu.make_async_copy(sbuf.at[own], rbuf.at[own], own_sem.at[k])

    def send(k, n, skip):
        for j, (core, z) in enumerate([(0, 0)] + LINE_PLACES):
            if j == skip:
                continue
            xy = lax.rem(n * 5 + j * 7, 16)
            device, to = neighbour(here, (xy // 4, lax.rem(xy, 4), core, z))
            size = GROUPS[k] * TILES
            pltpu.make_async_remote_copy(
                src_ref=sbuf.at[pl.ds((k * PEERS + to) * PITCH, size)],
                dst_ref=rbuf.at[pl.ds((k * PEERS + me) * PITCH, size)],
                send_sem=send_sem.at[k], recv_sem=recv_sem.at[k], device_id=device, device_id_type=MESH,
            ).start()

    column = lax.broadcasted_iota(jnp.int32, (1, 128), 1).astype(F32)

    def fill(n, _):
        r, block = n // (WIDTH // 128), lax.rem(n, WIDTH // 128)
        quarter = (lon_ref[r] // 4).astype(F32)
        inverse = 1.0 / quarter
        p = column + (block * 128).astype(F32)
        at = pl.multiple_of(block * 128, 128)
        for e in range(CHUNKS):
            for u in range(2):
                whole = (runs * 10.0 + (2 * e + u)) * p
                rest = whole - jnp.floor(whole * inverse) * quarter
                c, s = quarter_trig(rest * (4.0 * inverse))
                tab[r, pl.ds(e * 128 + u * 32, 32), pl.ds(at, 128)] = c.astype(BF16)
                tab[r, pl.ds(e * 128 + 64 + u * 32, 32), pl.ds(at, 128)] = s.astype(BF16)
        step = 4.0 / lon_ref[r].astype(F32)
        inside = jnp.where(p < quarter, 1.0, 0.0)
        kept = [inside]
        for g in range(1, 4):
            kept += quarter_trig(p * (g * step))
        for k, value in enumerate(kept):
            turn[r, pl.ds(k * 8, 8), pl.ds(at, 128)] = jnp.broadcast_to(value * inside, (8, 128))
        return 0

    tab_copy = pltpu.make_async_copy(tab, tab_hbm, tab_sem)
    turn_copy = pltpu.make_async_copy(turn, turn_hbm, turn_sem)

    wide = lax.broadcasted_iota(jnp.int32, (1, 128), 1)
    main_g = (wide // 32).astype(F32)
    tail_g = ((wide % 16) // 4).astype(F32)

    def out_copy(e):
        part = pl.ds(pl.multiple_of(e * 128, 128), 128)
        return pltpu.make_async_copy(lhs.at[:, :, part], lhs_hbm.at[:, :, part], out_sem.at[e])

    def take(e, _):
        def rows(core, z, tile):
            return rbuf[pl.ds(first_row(e) + (core * 4 + z) * 16 * PITCH + tile, 16, stride=PITCH), :]

        for r in range(2):
            longs = lon_ref[r].astype(F32)
            for u in range(2):
                m0 = (runs * 10.0 + (2 * e + u).astype(F32)) * 4.0
                m_main, m_tail = m0 + main_g, m0 + tail_g
                weight_main = jnp.where(2.0 * m_main < longs, jnp.where(m_main == 0.0, 1.0, 2.0), 0.0)
                weight_tail = jnp.where(2.0 * m_tail < longs, jnp.where(m_tail == 0.0, 1.0, 2.0), 0.0)
                for c in range(2):
                    i = r * 4 + c * 2 + u
                    picked = jnp.where(wide // 16 == i, weight_tail, 0.0)
                    at = r * 128 + c * 64 + u * 32
                    swapped = r * 128 + (1 - c) * 64 + u * 32
                    for z in range(4):
                        for kind, tile, weight in ((0, i, weight_main), (1, 8, picked)):
                            value = jnp.concatenate([rows(0, z, tile), rows(1, z, tile)], axis=0) * weight
                            lanes = pl.ds((kind * 4 + z) * 128, 128)
                            vmat[0, pl.ds(at, 32), lanes] = (value if c == 0 else -value).astype(BF16)
                            vmat[1, pl.ds(swapped, 32), lanes] = value.astype(BF16)
        part = pl.ds(pl.multiple_of(e * 128, 128), 128)
        for half in range(2):
            real = nt(perm[half], vmat[0]).astype(BF16)
            imag = nt(perm[half, pl.ds(HALF, IM_ROWS), :], vmat[1]).astype(BF16)
            for r in range(2):
                lhs[r * 2 + half, pl.ds(0, RE_ROWS), part] = real[:, r * 128 : (r + 1) * 128]
                lhs[r * 2 + half, pl.ds(RE_ROWS, IM_ROWS), part] = imag[:, r * 128 : (r + 1) * 128]
        out_copy(e).start()
        return 0

    def whole(k, sem):
        total = pl.ds(0, (PEERS - 1) * GROUPS[k] * TILES)
        return pltpu.make_async_copy(sbuf.at[total], rbuf.at[total], sem.at[k])

    blocks = 2 * (WIDTH // 128)
    done = 0
    for k in range(3):
        lax.fori_loop(2 * k, 2 * k + GROUPS[k], pack, 0)
        own_copy(k).start()
        send(k, 0, 0)
        filled = min(done + 15, blocks)

        def some(n, _):
            send(k, n, -1)
            fill(done + n - 1, 0)
            return 0

        def rest(n, _):
            send(k, n, -1)
            return 0

        lax.fori_loop(1, 1 + filled - done, some, 0)
        lax.fori_loop(1 + filled - done, 16, rest, 0)
        done = filled
    tab_copy.start()
    turn_copy.start()
    for k in range(3):
        whole(k, recv_sem).wait()
        own_copy(k).wait()
        lax.fori_loop(2 * k, 2 * k + GROUPS[k], take, 0)
    for k in range(3):
        whole(k, send_sem).wait()
    for e in range(CHUNKS):
        out_copy(e).wait()
    tab_copy.wait()
    turn_copy.wait()


def synthesis(
    lon_ref, lhs_hbm, tab_hbm, turn_hbm, out_hbm,
    lhs, tab, turn, z0, z1, parts0, parts1, out0, out1, lhs_sem, tab_sem, turn_sem, out_sem,
):
    sums, outs = (z0, z1), (out0, out1)

    def lhs_copy(s):
        return pltpu.make_async_copy(lhs_hbm.at[s], lhs.at[s], lhs_sem.at[s])

    def tab_copy(r):
        return pltpu.make_async_copy(tab_hbm.at[r], tab.at[r], tab_sem.at[r])

    def turn_copy(r):
        return pltpu.make_async_copy(turn_hbm.at[r], turn.at[r], turn_sem.at[r])

    def out_copy(s, third):
        rows = out_hbm.at[s // 2, pl.ds((s % 2) * HALF + third * 24, 24), :]
        return pltpu.make_async_copy(outs[s % 2].at[pl.ds(third * 24, 24), :], rows, out_sem.at[s % 2, third])

    tab_copy(0).start()
    lhs_copy(0).start()
    turn_copy(0).start()
    lhs_copy(1).start()
    tab_copy(1).start()
    turn_copy(1).start()
    lhs_copy(2).start()
    lhs_copy(3).start()
    for ref in sums:
        ref[:, WIDTH - 128 :] = jnp.zeros((ROWS, 128), F32)
    lane = lax.broadcasted_iota(jnp.int32, (8, 128), 1)

    def product(s, at, width):
        sums[s % 2][:, pl.ds(at, width)] = jnp.dot(
            lhs[s], tab[s // 2, :, pl.ds(at, width)], preferred_element_type=F32
        )

    def unit(s, b, parts):
        source, out, r = sums[s % 2], outs[s % 2], s // 2
        quarter = lon_ref[r] // 4
        rows = pl.ds(pl.multiple_of(b * 8, 8), 8)
        for j in range(WIDTH // 128):
            lanes = pl.ds(j * 128, 128)

            def get(row):
                return source[pl.ds(pl.multiple_of(row * HALF + b * 8, 8), 8), lanes]

            re0, re1, re2, re3, im1, im2, im3 = (get(k) for k in range(7))
            inside, c1, s1, c2, s2, c3, s3 = (turn[r, pl.ds(k * 8, 8), lanes] for k in range(7))
            a0 = re0 * inside
            a2 = c2 * re2 - s2 * im2
            r1, i1 = c1 * re1 - s1 * im1, c1 * im1 + s1 * re1
            r3, i3 = c3 * re3 - s3 * im3, c3 * im3 + s3 * re3
            plus, minus = a0 + a2, a0 - a2
            across, along = r1 + r3, i1 - i3
            for t, value in enumerate((plus + across, minus - along, plus - across, minus + along)):
                parts[pl.ds(t * 8, 8), lanes] = value
        for t in range(4):
            start = t * quarter
            first, shift = start // 128, lax.rem(start, 128)
            below = lane < shift
            before = out[rows, pl.ds(pl.multiple_of(first * 128, 128), 128)]
            previous = None
            for j in range(WIDTH // 128):
                turned = pltpu.roll(parts[pl.ds(t * 8, 8), pl.ds(j * 128, 128)], shift, axis=1)
                value = jnp.where(below, before, turned)
                before = turned
                if t == 3 and j == WIDTH // 128 - 1:
                    full = first == 30
                    out[rows, pl.ds(5120, 16)] = jnp.where(full, value, 0.0)[:, :16]
                    value = jnp.where(full, previous, value)
                    place_at = jnp.minimum(first + j, 39)
                else:
                    place_at = first + j
                out[rows, pl.ds(pl.multiple_of(place_at * 128, 128), 128)] = value
                previous = value

    for s in range(5):
        if s < 4:
            lhs_copy(s).wait()
            if s % 2 == 0:
                tab_copy(s // 2).wait()
        if s >= 1:
            if s % 2 == 1:
                turn_copy(s // 2).wait()
            if s >= 3:
                for third in range(3):
                    out_copy(s - 3, third).wait()
            out = outs[(s - 1) % 2]
            covered = (3 * (lon_ref[(s - 1) // 2] // 4)) // 128 + 11

            def clear(tile, _):
                out[:, pl.ds(pl.multiple_of(tile * 128, 128), 128)] = jnp.zeros((HALF, 128), F32)
                return 0

            lax.fori_loop(covered, 40, clear, 0)

        if s < 4:
            product(s, 0, 1280)
        if s >= 1:
            for b in range(HALF // 8):
                unit(s - 1, b, (parts0, parts1)[b % 2])
                if b % 3 == 2:
                    out_copy(s - 1, b // 3).start()
        if s < 4:

            @pl.when(lon_ref[s // 2] > 5120)
            def _():
                product(s, 1280, 128)

    for s in (2, 3):
        for third in range(3):
            out_copy(s, third).wait()


def on_device(legendre, spectral, slot_wave, band_rows, lon_count):
    perm = jnp.asarray(placement_matrix(), BF16)
    anywhere = pl.BlockSpec(memory_space=pl.ANY)
    smem = pl.BlockSpec(memory_space=pltpu.SMEM)
    dma = pltpu.SemaphoreType.DMA
    n_gather = len(PLANE) + len(LINE)
    lhs, tab, turn = pl.pallas_call(
        exchange,
        out_shape=(
            jax.ShapeDtypeStruct((4, ROWS, 640), BF16),
            jax.ShapeDtypeStruct((2, 640, WIDTH), BF16),
            jax.ShapeDtypeStruct((2, TURNS, WIDTH), F32),
        ),
        in_specs=[smem, smem, smem, anywhere, anywhere, anywhere],
        out_specs=(anywhere, anywhere, anywhere),
        scratch_shapes=[
            pltpu.VMEM((SLOTS, DEPTH, NORTH), BF16),
            pltpu.VMEM((SLOTS, COLS, DEPTH), BF16),
            pltpu.VMEM((2, RE_ROWS, 1024), BF16),
            pltpu.VMEM((4, 160, DEPTH), BF16),
            pltpu.VMEM((SLOTS * COLS, 128), F32),
            pltpu.VMEM((SLOTS * COLS, 128), F32),
            pltpu.VMEM((PEERS, 1, 128), F32),
            pltpu.VMEM((SLOTS, 128), jnp.int32),
            pltpu.SMEM((SLOTS, 128), jnp.int32),
            pltpu.VMEM((2, PEERS, 256), BF16),
            pltpu.VMEM((len(GROUPS) * PEERS * PITCH, 128), F32),
            pltpu.VMEM((len(GROUPS) * PEERS * PITCH, 128), F32),
            pltpu.VMEM((2, 256, 1024), BF16),
            pltpu.VMEM((4, ROWS, 640), BF16),
            pltpu.VMEM((2, 640, WIDTH), BF16),
            pltpu.VMEM((2, TURNS, WIDTH), F32),
            dma((CHUNKS, 2)),
            dma,
            dma,
            dma((n_gather,)),
            dma((n_gather,)),
            dma((len(GROUPS),)),
            dma((len(GROUPS),)),
            dma((len(GROUPS),)),
            dma((CHUNKS,)),
            dma,
            dma,
        ],
        compiler_params=pltpu.CompilerParams(collective_id=0, has_side_effects=True, vmem_limit_bytes=58 << 20),
    )(band_rows, lon_count, slot_wave, legendre, jnp.swapaxes(spectral, 1, 2), perm)
    return pl.pallas_call(
        synthesis,
        out_shape=jax.ShapeDtypeStruct((2, FIELDS, LONS), F32),
        in_specs=[smem, anywhere, anywhere, anywhere],
        out_specs=anywhere,
        scratch_shapes=[
            pltpu.VMEM((4, ROWS, 640), BF16),
            pltpu.VMEM((2, 640, WIDTH), BF16),
            pltpu.VMEM((2, TURNS, WIDTH), F32),
            pltpu.VMEM((ROWS, WIDTH), F32),
            pltpu.VMEM((ROWS, WIDTH), F32),
            pltpu.VMEM((32, WIDTH), F32),
            pltpu.VMEM((32, WIDTH), F32),
            pltpu.VMEM((HALF, LONS), F32),
            pltpu.VMEM((HALF, LONS), F32),
            dma((4,)),
            dma((2,)),
            dma((2,)),
            dma((2, 3)),
        ],
        compiler_params=pltpu.CompilerParams(vmem_limit_bytes=58 << 20),
    )(lon_count, lhs, tab, turn)


def solution(mesh):
    return jax.shard_map(
        on_device,
        mesh=mesh,
        in_specs=(
            P("wave", None, None),
            P("wave", None, "lev"),
            P("wave"),
            P(("wave", "lev")),
            P(("wave", "lev")),
        ),
        out_specs=P(("wave", "lev"), None, None),
        check_vma=False,
    )
```
